256 devices in a mesh: fam: 8 (over y_hi, x), owner: 32 (over y_lo, z, core).
Axes of the slice: x: 4, y: 4 (y_hi: 2, y_lo: 2; y = y_hi * 2 + y_lo), z: 8, core: 2. Of those that a mesh axis runs over, the one named last changes fastest.
Arguments:
- wavefunction: bfloat16 [16384, 512], P('owner'), may hold values from -6 to 6
- left_blocks: bfloat16 [8, 8, 16384, 1024], P('fam', None, 'owner'), may hold values from -0.1875 to 0.1875
- right_blocks: bfloat16 [8, 512, 512], P('fam'), may hold values from -0.0625 to 0.0625
- term_sources: int32 [8, 16, 8], replicated, may hold values from 0 to 15
- term_counts: int32 [8, 16], replicated, may hold values from 1 to 8, as said below
- sector_rows: int32 [16], replicated, may hold values from 256 to 1024
Outputs:
- sigma: bfloat16 [16384, 512], P('owner', 'fam')
The draws below stay inside these ranges and needn't reach their ends.
Inputs may be any that keep to these rules, and one draw needn't show every extreme that they name: `term_counts`: every entry lies in 1 to 8; for every output sector some family has exactly 8 live slots.
All inputs are finite; a program needn't handle non-finite values.
Results may differ from the reference program's by a relative error of at most 0.0095.
Values may be sent and summed in bfloat16 or wider, within the bound.
A program may use at most 128 MiB of HBM per device.

```python
import jax
import jax.numpy as jnp
from jax import lax

S = 16
SROW = 1024
COLS = 512
KMAX = 8
FAM = 8
BOND = 16384
N_FAM = 8


def draw_term_counts(key, part):
    base = jax.random.fold_in(key, 7)
    first_key, second_key, third_key = jax.random.split(base, 3)
    first = jax.random.randint(first_key, (FAM, S), 0, KMAX)
    second = jax.random.randint(second_key, (FAM, S), 0, KMAX)
    counted = 1 + first * second // (KMAX - 1)
    busiest = jax.random.randint(third_key, (S,), 0, FAM)
    family = jnp.arange(FAM, dtype=jnp.int32)
    counted = jnp.where(family[:, None] == busiest[None, :], KMAX, counted)
    return counted.astype(jnp.int32)


def set_ends(drawn, rng, least, high):
    longest = drawn.shape.index(max(drawn.shape))
    spots = []
    for shift in (0, 1):
        where = [jax.random.randint(jax.random.fold_in(rng, axis), (), 0, length) for axis, length in enumerate(drawn.shape)]
        where[longest] = (where[longest] + shift) % drawn.shape[longest]
        spots.append(tuple(where))
    return drawn.at[spots[0]].set(least).at[spots[1]].set(high)


def levels(own_key, shape, cuts, least, largest):
    gain, own = 1.0, jax.random.fold_in(own_key, 6)
    for dim, shards_of in cuts:
        steps = jnp.exp(jax.random.uniform(jax.random.fold_in(own, dim), (shards_of,), jnp.float32, least / len(cuts), largest / len(cuts)))
        gain = gain * jnp.repeat(steps, shape[dim] // shards_of).reshape([-1 if axis == dim else 1 for axis in range(len(shape))])
    return gain


def scatter_about(key, dims, deviation, limit, shards=(), kind=jnp.bfloat16):
    array = deviation * jax.random.normal(key, dims, jnp.float32)
    if shards:
        array = array * levels(key, dims, shards, -0.22, 0.18)
    return jnp.clip(array, -limit, limit).astype(kind)


def setup_inputs(seed: int = 0) -> dict:
    key_list = jax.random.split(jax.random.key(seed), 7)
    wavefunction = scatter_about(key_list[0], (BOND, COLS), 1.0, 6.0, ((0, 32),))
    left_blocks = scatter_about(key_list[1], (FAM, KMAX, BOND, SROW), SROW ** -0.5, 0.1875, ((0, 8), (2, 32)))
    right_blocks = scatter_about(key_list[2], (FAM, COLS, COLS), (16 * COLS) ** -0.5, 0.0625, ((0, 8),))
    term_sources = set_ends(jax.random.randint(key_list[3], (FAM, S, KMAX), 0, S), jax.random.fold_in(key_list[3], 1), 0, S - 1).astype(jnp.int32)
    term_counts = draw_term_counts(jax.random.fold_in(key_list[6], 71), 0)
    sector_rows = set_ends(jax.random.randint(key_list[5], (S,), SROW // 4, SROW + 1), jax.random.fold_in(key_list[5], 1), SROW // 4, SROW).astype(jnp.int32)
    return dict(wavefunction=wavefunction, left_blocks=left_blocks, right_blocks=right_blocks, term_sources=term_sources, term_counts=term_counts, sector_rows=sector_rows)


def row_mask(sector_rows):
    rows = jnp.arange(S * SROW, dtype=jnp.int32)
    sector = rows // SROW
    return (rows % SROW) < sector_rows[sector]


def reference(wavefunction, left_blocks, right_blocks, term_sources, term_counts, sector_rows):
    keep = row_mask(sector_rows)
    masked = jnp.where(keep[:, None], wavefunction, jnp.zeros_like(wavefunction))
    stacked = masked.reshape(S, SROW, COLS)

    def one_sector(target):
        def family_step(total, family):
            def slot_step(total, slot):
                live = slot < term_counts[family, target]

                def add_term(running):
                    left = lax.dynamic_slice(left_blocks, (family, slot, target * SROW, jnp.int32(0)), (1, 1, SROW, SROW))[0, 0]
                    source = stacked[term_sources[family, target, slot]]
                    partial_value = jnp.dot(left, source, preferred_element_type=jnp.float32).astype(jnp.bfloat16)
                    return running + jnp.dot(partial_value, right_blocks[family], preferred_element_type=jnp.float32)

                def keep_same(running):
                    return running

                return lax.cond(live, add_term, keep_same, total), None

            total, _ = lax.scan(slot_step, total, jnp.arange(KMAX, dtype=jnp.int32))
            return total, None

        total, _ = lax.scan(family_step, jnp.zeros((SROW, COLS), jnp.float32), jnp.arange(N_FAM, dtype=jnp.int32))
        return total

    totals = lax.map(one_sector, jnp.arange(S, dtype=jnp.int32)).reshape(S * SROW, COLS)
    return jnp.where(keep[:, None], totals, jnp.zeros_like(totals)).astype(jnp.bfloat16)
```

```python
import functools

import jax
import jax.numpy as jnp
from jax import lax
from jax.experimental import pallas as pl
from jax.experimental.pallas import tpu as pltpu
from jax.sharding import PartitionSpec as P

MESH = pl.DeviceIdType.MESH
S, SROW, COLS, KMAX, FAM = 16, 1024, 512, 8, 8
ROWS = 512
GROUPS = 2
CHUNK = ROWS // (4 * GROUPS)
LAG = 3
SPLIT_OWN, SPLIT_OPPOSITE = 8, 10
PARTS = 2
LINKS = ("z+", "z-", "y+", "y-", "x+", "x-")


def sender_label(link, label):
    dq, dz, h, j = label
    if link == "z+":
        return (0, dz - 1, h, j)
    if link == "z-":
        return (0, -3 if dz == 4 else dz + 1, h, j)
    if link[0] == "y":
        return (0, dz, h, j)
    if link == "x+":
        return (dq, dz, h, (j - 1) % 4)
    return (dq, dz, h, (j + 1) % 4)


def schedule():
    own = [(dz, h) for dz in (-1, 1, -2, 2, -3, 3, 4) for h in range(GROUPS)][:SPLIT_OWN]
    opposite = [(dz, h) for dz in (0, -1, 1, -2, 2, -3, 3, 4) for h in range(GROUPS)][:SPLIT_OPPOSITE]
    arrived = {(0, 0, h, j): -LAG for h in range(GROUPS) for j in range(4)}
    todo = {}
    for dq in (0, 1):
        for dz in range(-3, 5):
            if (dq, dz) == (0, 0):
                continue
            for h in range(GROUPS):
                split = (dz, h) in (opposite if dq else own)
                for j in range(4):
                    if split and j % 2:
                        links = ("x+",) if j == 1 else ("x-",)
                    elif dq:
                        links = ("y+", "y-")
                    elif dz == 4:
                        links = ("z+", "z-")
                    else:
                        links = ("z+",) if dz > 0 else ("z-",)
                    todo[(dq, dz, h, j)] = links

    def order(label):
        dq, dz, h, j = label
        ahead = 0
        if dq == 0:
            ahead += (4 - abs(dz)) * 10 + 3
        if j == 0 and (dz, h) in (opposite if dq else own):
            ahead += 2
        if dq == 0 and (dz, h) in opposite:
            ahead += 2
        return (-ahead, abs(dz), h, j)

    rounds = []
    while todo:
        now = {}
        for link in LINKS:
            ready = [
                label
                for label, links in todo.items()
                if link in links and arrived.get(sender_label(link, label), 1 << 20) <= len(rounds) - LAG
            ]
            if ready:
                now[link] = min(ready, key=order)
                del todo[now[link]]
        for label in now.values():
            arrived[label] = len(rounds)
        rounds.append(now)
    return rounds


ROUNDS = schedule()


def kernel(
    sources_ref,
    counts_ref,
    used_ref,
    wave_hbm,
    left_hbm,
    right_hbm,
    out_ref,
    gathered,
    wave,
    left,
    right,
    right_t,
    sums,
    outgoing,
    incoming,
    load_sem,
    send_sem,
    recv_sem,
    core_send_sem,
    core_recv_sem,
    fam_send_sem,
    fam_recv_sem,
):
    f = lax.axis_index("fam")
    o = lax.axis_index("owner")
    x, yh = lax.rem(f, 4), f // 4
    core, z, yl = lax.rem(o, 2), lax.rem(o // 2, 8), o // 16
    y = yh * 2 + yl
    sector = o // 2

    def device(dx, dy, dz, other=False):
        nx, ny, nz = lax.rem(x + dx + 4, 4), lax.rem(y + dy + 4, 4), lax.rem(z + dz + 8, 8)
        c = 1 - core if other else core
        return ((ny // 2) * 4 + nx, (lax.rem(ny, 2) * 8 + nz) * 2 + c)

    loads = [
        pltpu.make_async_copy(wave_hbm, wave, load_sem.at[0]),
        pltpu.make_async_copy(right_hbm, right, load_sem.at[1]),
        pltpu.make_async_copy(left_hbm, left, load_sem.at[2]),
    ]
    for load in loads:
        load.start()

    barrier = pltpu.get_barrier_semaphore()
    fam_steps = [(dx, dy) for dy in (0, 2) for dx in range(4) if (dx, dy) != (0, 0)]
    greeted = [(dx, dy, 0, False) for dx, dy in fam_steps]
    greeted += [(0, 1, 0, False), (0, -1, 0, False), (0, 0, 1, False), (0, 0, -1, False), (0, 0, 0, True)]
    for where in greeted:
        pl.semaphore_signal(barrier, inc=1, device_id=device(*where), device_id_type=MESH)

    def chunk_at(label):
        dq, dz, h, j = label
        q = 1 - yl if dq else yl
        a = q * 8 + lax.rem(z + dz + 8, 8)
        i = 4 * h + lax.rem(x + j, 4)
        return gathered.at[a, pl.ds(pl.multiple_of(core * ROWS + i * CHUNK, CHUNK), CHUNK)]

    own = pl.ds(pl.multiple_of(core * ROWS, ROWS), ROWS)
    used_here = used_ref[sector] - core * ROWS
    loads[0].wait()
    row = lax.broadcasted_iota(jnp.int32, (ROWS, COLS), 0)
    gathered[sector, own, :] = jnp.where(row < used_here, wave[...].astype(jnp.float32), 0.0).astype(jnp.bfloat16)

    pl.semaphore_wait(barrier, len(greeted))

    targets = {
        "z+": (0, 0, -1), "z-": (0, 0, 1), "y+": (0, -1, 0), "y-": (0, 1, 0), "x+": (-1, 0, 0), "x-": (1, 0, 0),
    }

    def to_other_core(part):
        pltpu.make_async_remote_copy(
            src_ref=part, dst_ref=part, send_sem=core_send_sem, recv_sem=core_recv_sem,
            device_id=device(0, 0, 0, True), device_id_type=MESH,
        ).start()

    for step in range(len(ROUNDS) + LAG):
        if step >= LAG:
            for link, label in ROUNDS[step - LAG].items():
                part = chunk_at(label)
                pltpu.make_async_remote_copy(
                    src_ref=part, dst_ref=part, send_sem=send_sem, recv_sem=recv_sem.at[step - LAG, LINKS.index(link)],
                    device_id=device(*targets[link]), device_id_type=MESH,
                ).wait_recv()
        if step < len(ROUNDS):
            for link, label in ROUNDS[step].items():
                part = chunk_at(sender_label(link, label))
                pltpu.make_async_remote_copy(
                    src_ref=part, dst_ref=part, send_sem=send_sem, recv_sem=recv_sem.at[step, LINKS.index(link)],
                    device_id=device(*targets[link]), device_id_type=MESH,
                ).start()
        if step == 0:
            to_other_core(gathered.at[sector, own])
            loads[1].wait()
            right_t[...] = right[0].astype(jnp.float32).T.astype(jnp.bfloat16)
        if step >= LAG:
            for label in ROUNDS[step - LAG].values():
                to_other_core(chunk_at(label))
    loads[2].wait()
    half = gathered.at[pl.ds(0, S // 2)]
    pltpu.make_async_copy(half, half, core_recv_sem).wait()

    live_slots = counts_ref[f, sector]
    depth = ROWS // PARTS
    for part in range(PARTS):

        def add_slot(k, carry, part=part):
            a = sources_ref[f, k, sector]
            product = jnp.dot(
                left[0, k, part * depth : (part + 1) * depth, :],
                gathered[a],
                preferred_element_type=jnp.float32,
            )
            slot = k + jnp.zeros((depth, COLS), jnp.int32)
            sums[...] += jnp.where(slot < live_slots, product, 0.0)
            return carry

        sums[...] = jnp.zeros_like(sums)
        lax.fori_loop(0, KMAX, add_slot, 0)
        turned = lax.dot_general(
            right_t[...], sums[...].astype(jnp.bfloat16), (((1,), (1,)), ((), ())), preferred_element_type=jnp.float32
        )
        outgoing[part] = turned.astype(jnp.bfloat16).reshape(FAM, COLS // FAM, depth)
        for dx, dy in fam_steps:
            there = device(dx, dy, 0)
            pltpu.make_async_remote_copy(
                src_ref=outgoing.at[part, there[0]], dst_ref=incoming.at[part, f], send_sem=fam_send_sem,
                recv_sem=fam_recv_sem.at[part], device_id=there, device_id_type=MESH,
            ).start()

    for part in range(PARTS):
        others = incoming.at[part, pl.ds(0, FAM - 1)]
        pltpu.make_async_copy(others, others, fam_recv_sem.at[part]).wait()
        incoming[part, f] = outgoing[part, f]
        total = jnp.sum(incoming[part].astype(jnp.float32), axis=0)
        column = part * depth + lax.broadcasted_iota(jnp.int32, total.shape, 1)
        out_ref[:, part * depth : (part + 1) * depth] = jnp.where(column < used_here, total, 0.0).astype(jnp.bfloat16)

    for part in range(PARTS):
        others = outgoing.at[part, pl.ds(0, FAM - 1)]
        pltpu.make_async_copy(others, others, fam_send_sem).wait()
    sent = gathered.at[pl.ds(0, S - 1), pl.ds(0, ROWS)]
    pltpu.make_async_copy(sent, sent, send_sem).wait()
    pltpu.make_async_copy(half, half, core_send_sem).wait()


def body(wavefunction, left_blocks, right_blocks, term_sources, term_counts, sector_rows):
    vmem = pl.BlockSpec(memory_space=pltpu.VMEM)
    smem = pl.BlockSpec(memory_space=pltpu.SMEM)
    anywhere = pl.BlockSpec(memory_space=pl.ANY)
    turned = pl.pallas_call(
        kernel,
        out_shape=jax.ShapeDtypeStruct((COLS // FAM, ROWS), jnp.bfloat16),
        in_specs=[smem, smem, smem, anywhere, anywhere, anywhere],
        out_specs=vmem,
        scratch_shapes=[
            pltpu.VMEM((S, SROW, COLS), jnp.bfloat16),
            pltpu.VMEM((ROWS, COLS), jnp.bfloat16),
            pltpu.VMEM((1, KMAX, ROWS, SROW), jnp.bfloat16),
            pltpu.VMEM((1, COLS, COLS), jnp.bfloat16),
            pltpu.VMEM((COLS, COLS), jnp.bfloat16),
            pltpu.VMEM((ROWS // PARTS, COLS), jnp.float32),
            pltpu.VMEM((PARTS, FAM, COLS // FAM, ROWS // PARTS), jnp.bfloat16),
            pltpu.VMEM((PARTS, FAM, COLS // FAM, ROWS // PARTS), jnp.bfloat16),
            pltpu.SemaphoreType.DMA((3,)),
            pltpu.SemaphoreType.DMA,
            pltpu.SemaphoreType.DMA((len(ROUNDS), len(LINKS))),
            pltpu.SemaphoreType.DMA,
            pltpu.SemaphoreType.DMA,
            pltpu.SemaphoreType.DMA,
            pltpu.SemaphoreType.DMA((PARTS,)),
        ],
        compiler_params=pltpu.CompilerParams(
            collective_id=0, has_side_effects=True, vmem_limit_bytes=56 * 2**20
        ),
        cost_estimate=pl.CostEstimate(flops=2 * KMAX * ROWS * SROW * COLS, bytes_accessed=9 * 2**20, transcendentals=0),
        name="gather_multiply_scatter",
    )(jnp.swapaxes(term_sources, 1, 2), term_counts, sector_rows, wavefunction, left_blocks, right_blocks)
    return turned.T


def solution(mesh):
    return jax.shard_map(
        body,
        mesh=mesh,
        in_specs=(
            P("owner", None),
            P("fam", None, "owner", None),
            P("fam", None, None),
            P(),
            P(),
            P(),
        ),
        out_specs=P("owner", "fam"),
        check_vma=False,
    )
```

```python
import functools

import jax
import jax.numpy as jnp
from jax import lax
from jax.experimental import pallas as pl
from jax.experimental.pallas import tpu as pltpu
from jax.sharding import PartitionSpec as P

MESH = pl.DeviceIdType.MESH
S, SROW, COLS, KMAX, FAM = 16, 1024, 512, 8, 8
ROWS = 512
GROUPS = 2
CHUNK = ROWS // (4 * GROUPS)
LAG = 4
SPLIT_OWN, SPLIT_OPPOSITE = 8, 10
PARTS = 2
LINKS = ("z+", "z-", "y+", "y-", "x+", "x-")


def sender_label(link, label):
    dq, dz, h, j = label
    if link == "z+":
        return (0, dz - 1, h, j)
    if link == "z-":
        return (0, -3 if dz == 4 else dz + 1, h, j)
    if link[0] == "y":
        return (0, dz, h, j)
    if link == "x+":
        return (dq, dz, h, (j - 1) % 4)
    return (dq, dz, h, (j + 1) % 4)


def schedule():
    own = [(dz, h) for dz in (-1, 1, -2, 2, -3, 3, 4) for h in range(GROUPS)][:SPLIT_OWN]
    opposite = [(dz, h) for dz in (0, -1, 1, -2, 2, -3, 3, 4) for h in range(GROUPS)][:SPLIT_OPPOSITE]
    arrived = {(0, 0, h, j): -LAG for h in range(GROUPS) for j in range(4)}
    todo = {}
    for dq in (0, 1):
        for dz in range(-3, 5):
            if (dq, dz) == (0, 0):
                continue
            for h in range(GROUPS):
                split = (dz, h) in (opposite if dq else own)
                for j in range(4):
                    if split and j % 2:
                        links = ("x+",) if j == 1 else ("x-",)
                    elif dq:
                        links = ("y+", "y-")
                    elif dz == 4:
                        links = ("z+", "z-")
                    else:
                        links = ("z+",) if dz > 0 else ("z-",)
                    todo[(dq, dz, h, j)] = links

    def order(label):
        dq, dz, h, j = label
        ahead = 0
        if dq == 0:
            ahead += (4 - abs(dz)) * 10 + 3
        if j == 0 and (dz, h) in (opposite if dq else own):
            ahead += 2
        if dq == 0 and (dz, h) in opposite:
            ahead += 2
        return (-ahead, abs(dz), h, j)

    rounds = []
    while todo:
        now = {}
        for link in LINKS:
            ready = [
                label
                for label, links in todo.items()
                if link in links and arrived.get(sender_label(link, label), 1 << 20) <= len(rounds) - LAG
            ]
            if ready:
                now[link] = min(ready, key=order)
                del todo[now[link]]
        for label in now.values():
            arrived[label] = len(rounds)
        rounds.append(now)
    return rounds


ROUNDS = schedule()


def kernel(
    sources_ref,
    counts_ref,
    used_ref,
    wave_hbm,
    left_hbm,
    right_hbm,
    out_ref,
    gathered,
    wave,
    left,
    right,
    right_t,
    sums,
    outgoing,
    incoming,
    load_sem,
    send_sem,
    recv_sem,
    core_send_sem,
    core_recv_sem,
    fam_send_sem,
    fam_recv_sem,
):
    f = lax.axis_index("fam")
    o = lax.axis_index("owner")
    x, yh = lax.rem(f, 4), f // 4
    core, z, yl = lax.rem(o, 2), lax.rem(o // 2, 8), o // 16
    y = yh * 2 + yl
    sector = o // 2

    def device(dx, dy, dz, other=False):
        nx, ny, nz = lax.rem(x + dx + 4, 4), lax.rem(y + dy + 4, 4), lax.rem(z + dz + 8, 8)
        c = 1 - core if other else core
        return ((ny // 2) * 4 + nx, (lax.rem(ny, 2) * 8 + nz) * 2 + c)

    loads = [
        pltpu.make_async_copy(wave_hbm, wave, load_sem.at[0]),
        pltpu.make_async_copy(right_hbm, right, load_sem.at[1]),
        pltpu.make_async_copy(left_hbm, left, load_sem.at[2]),
    ]
    for load in loads:
        load.start()

    barrier = pltpu.get_barrier_semaphore()
    fam_steps = [(dx, dy) for dy in (0, 2) for dx in range(4) if (dx, dy) != (0, 0)]
    greeted = [(dx, dy, 0, False) for dx, dy in fam_steps]
    greeted += [(0, 1, 0, False), (0, -1, 0, False), (0, 0, 1, False), (0, 0, -1, False), (0, 0, 0, True)]
    for where in greeted:
        pl.semaphore_signal(barrier, inc=1, device_id=device(*where), device_id_type=MESH)

    def chunk_at(label):
        dq, dz, h, j = label
        q = 1 - yl if dq else yl
        a = q * 8 + lax.rem(z + dz + 8, 8)
        i = 4 * h + lax.rem(x + j, 4)
        return gathered.at[a, pl.ds(pl.multiple_of(core * ROWS + i * CHUNK, CHUNK), CHUNK)]

    own = pl.ds(pl.multiple_of(core * ROWS, ROWS), ROWS)
    used_here = used_ref[sector] - core * ROWS
    loads[0].wait()
    row = lax.broadcasted_iota(jnp.int32, (ROWS, COLS), 0)
    gathered[sector, own, :] = jnp.where(row < used_here, wave[...].astype(jnp.float32), 0.0).astype(jnp.bfloat16)

    pl.semaphore_wait(barrier, len(greeted))

    targets = {
        "z+": (0, 0, -1), "z-": (0, 0, 1), "y+": (0, -1, 0), "y-": (0, 1, 0), "x+": (-1, 0, 0), "x-": (1, 0, 0),
    }

    def to_other_core(part):
        pltpu.make_async_remote_copy(
            src_ref=part, dst_ref=part, send_sem=core_send_sem, recv_sem=core_recv_sem,
            device_id=device(0, 0, 0, True), device_id_type=MESH,
        ).start()

    for step in range(len(ROUNDS) + LAG):
        if step >= LAG:
            for link, label in ROUNDS[step - LAG].items():
                part = chunk_at(label)
                pltpu.make_async_remote_copy(
                    src_ref=part, dst_ref=part, send_sem=send_sem, recv_sem=recv_sem.at[step - LAG, LINKS.index(link)],
                    device_id=device(*targets[link]), device_id_type=MESH,
                ).wait_recv()
        if step < len(ROUNDS):
            for link, label in ROUNDS[step].items():
                part = chunk_at(sender_label(link, label))
                pltpu.make_async_remote_copy(
                    src_ref=part, dst_ref=part, send_sem=send_sem, recv_sem=recv_sem.at[step, LINKS.index(link)],
                    device_id=device(*targets[link]), device_id_type=MESH,
                ).start()
        if step == 0:
            to_other_core(gathered.at[sector, own])
            loads[1].wait()
            right_t[...] = right[0].astype(jnp.float32).T.astype(jnp.bfloat16)
        if step >= LAG:
            for label in ROUNDS[step - LAG].values():
                to_other_core(chunk_at(label))
    loads[2].wait()
    half = gathered.at[pl.ds(0, S // 2)]
    pltpu.make_async_copy(half, half, core_recv_sem).wait()

    live_slots = counts_ref[f, sector]
    depth = ROWS // PARTS
    for part in range(PARTS):

        def add_slot(k, carry, part=part):
            a = sources_ref[f, k, sector]
            product = jnp.dot(
                left[0, k, part * depth : (part + 1) * depth, :],
                gathered[a],
                preferred_element_type=jnp.float32,
            )
            slot = k + jnp.zeros((depth, COLS), jnp.int32)
            sums[...] += jnp.where(slot < live_slots, product, 0.0)
            return carry

        sums[...] = jnp.zeros_like(sums)
        lax.fori_loop(0, KMAX, add_slot, 0, unroll=True)
        turned = lax.dot_general(
            right_t[...], sums[...].astype(jnp.bfloat16), (((1,), (1,)), ((), ())), preferred_element_type=jnp.float32
        )
        outgoing[part] = turned.astype(jnp.bfloat16).reshape(FAM, COLS // FAM, depth)
        for dx, dy in fam_steps:
            there = device(dx, dy, 0)
            pltpu.make_async_remote_copy(
                src_ref=outgoing.at[part, there[0]], dst_ref=incoming.at[part, f], send_sem=fam_send_sem,
                recv_sem=fam_recv_sem.at[part], device_id=there, device_id_type=MESH,
            ).start()

    for part in range(PARTS):
        others = incoming.at[part, pl.ds(0, FAM - 1)]
        pltpu.make_async_copy(others, others, fam_recv_sem.at[part]).wait()
        incoming[part, f] = outgoing[part, f]
        total = jnp.sum(incoming[part].astype(jnp.float32), axis=0)
        column = part * depth + lax.broadcasted_iota(jnp.int32, total.shape, 1)
        out_ref[:, part * depth : (part + 1) * depth] = jnp.where(column < used_here, total, 0.0).astype(jnp.bfloat16)

    for part in range(PARTS):
        others = outgoing.at[part, pl.ds(0, FAM - 1)]
        pltpu.make_async_copy(others, others, fam_send_sem).wait()
    sent = gathered.at[pl.ds(0, S - 1), pl.ds(0, ROWS)]
    pltpu.make_async_copy(sent, sent, send_sem).wait()
    pltpu.make_async_copy(half, half, core_send_sem).wait()


def body(wavefunction, left_blocks, right_blocks, term_sources, term_counts, sector_rows):
    vmem = pl.BlockSpec(memory_space=pltpu.VMEM)
    smem = pl.BlockSpec(memory_space=pltpu.SMEM)
    anywhere = pl.BlockSpec(memory_space=pl.ANY)
    turned = pl.pallas_call(
        kernel,
        out_shape=jax.ShapeDtypeStruct((COLS // FAM, ROWS), jnp.bfloat16),
        in_specs=[smem, smem, smem, anywhere, anywhere, anywhere],
        out_specs=vmem,
        scratch_shapes=[
            pltpu.VMEM((S, SROW, COLS), jnp.bfloat16),
            pltpu.VMEM((ROWS, COLS), jnp.bfloat16),
            pltpu.VMEM((1, KMAX, ROWS, SROW), jnp.bfloat16),
            pltpu.VMEM((1, COLS, COLS), jnp.bfloat16),
            pltpu.VMEM((COLS, COLS), jnp.bfloat16),
            pltpu.VMEM((ROWS // PARTS, COLS), jnp.float32),
            pltpu.VMEM((PARTS, FAM, COLS // FAM, ROWS // PARTS), jnp.bfloat16),
            pltpu.VMEM((PARTS, FAM, COLS // FAM, ROWS // PARTS), jnp.bfloat16),
            pltpu.SemaphoreType.DMA((3,)),
            pltpu.SemaphoreType.DMA,
            pltpu.SemaphoreType.DMA((len(ROUNDS), len(LINKS))),
            pltpu.SemaphoreType.DMA,
            pltpu.SemaphoreType.DMA,
            pltpu.SemaphoreType.DMA,
            pltpu.SemaphoreType.DMA((PARTS,)),
        ],
        compiler_params=pltpu.CompilerParams(
            collective_id=0, has_side_effects=True, vmem_limit_bytes=56 * 2**20
        ),
        cost_estimate=pl.CostEstimate(flops=2 * KMAX * ROWS * SROW * COLS, bytes_accessed=9 * 2**20, transcendentals=0),
        name="gather_multiply_scatter",
    )(jnp.swapaxes(term_sources, 1, 2), term_counts, sector_rows, wavefunction, left_blocks, right_blocks)
    return turned.T


def solution(mesh):
    return jax.shard_map(
        body,
        mesh=mesh,
        in_specs=(
            P("owner", None),
            P("fam", None, "owner", None),
            P("fam", None, None),
            P(),
            P(),
            P(),
        ),
        out_specs=P("owner", "fam"),
        check_vma=False,
    )
```

```python
import functools

import jax
import jax.numpy as jnp
from jax import lax
from jax.experimental import pallas as pl
from jax.experimental.pallas import tpu as pltpu
from jax.sharding import PartitionSpec as P

MESH = pl.DeviceIdType.MESH
S, SROW, COLS, KMAX, FAM = 16, 1024, 512, 8, 8
ROWS = 512
GROUPS = 2
CHUNK = ROWS // (4 * GROUPS)
LAG = 3
PARTS = 2
DEPTH = ROWS // PARTS
LINKS = ((0, 0, 1), (0, 0, -1), (0, 1, 0), (0, -1, 0), (1, 0, 0), (-1, 0, 0))

ROUNDS = (
    (36, 20, 95, 92, -1, -1),
    (33, 18, 88, 89, -1, -1),
    (32, 16, 90, 94, -1, -1),
    (38, 84, 100, 91, 93, 39),
    (34, 10, 82, 97, 19, 17),
    (44, 21, 80, 96, 37, 35),
    (41, 23, 103, 102, 101, 87),
    (40, 12, 98, 74, 85, 81),
    (43, 2, 83, 99, 11, 47),
    (45, 8, 105, 108, 22, 9),
    (49, 4, 104, 76, 13, 86),
    (109, 15, 107, 66, 75, 46),
    (48, 14, 73, 72, 42, 111),
    (110, 60, 113, 77, 5, 7),
    (54, 0, 68, 79, 50, 106),
    (56, 64, 78, 112, 67, 51),
    (116, 3, 69, 124, 6, 1),
    (62, 58, 114, 71, 55, 63),
    (53, 70, 120, 115, 65, 59),
    (57, 122, 52, 118, 117, 119),
    (121, 123, 126, 127, 125, 61),
)


def parts_of(label):
    return label // 64, label // 8 % 8 - 3, label // 4 % 2, label % 4


def sender_parts(link, label):
    dq, dz, h, j = parts_of(label)
    dx, dy, step = LINKS[link]
    return (dq + dy) % 2, (dz - step + 3) % 8 - 3, h, (j - dx) % 4


def kernel(
    sources_ref,
    counts_ref,
    used_ref,
    wave_hbm,
    left_hbm,
    right_hbm,
    out_ref,
    gathered,
    left,
    right,
    right_t,
    sums,
    half_out,
    half_in,
    outgoing,
    incoming,
    load_sem,
    send_sem,
    recv_sem,
    left_send_sem,
    left_recv_sem,
    half_send_sem,
    half_recv_sem,
    fam_send_sem,
    fam_recv_sem,
):
    f = lax.axis_index("fam")
    o = lax.axis_index("owner")
    x, yh = lax.rem(f, 4), f // 4
    core, z, yl = lax.rem(o, 2), lax.rem(o // 2, 8), o // 16
    y = yh * 2 + yl
    sector = o // 2

    def device(dx, dy, dz, other=False):
        nx, ny, nz = lax.rem(x + dx + 4, 4), lax.rem(y + dy + 4, 4), lax.rem(z + dz + 8, 8)
        c = 1 - core if other else core
        return ((ny // 2) * 4 + nx, (lax.rem(ny, 2) * 8 + nz) * 2 + c)

    mine = pl.ds(pl.multiple_of(core * ROWS, ROWS), ROWS)
    others = pl.ds(pl.multiple_of((1 - core) * ROWS, ROWS), ROWS)
    loads = [
        pltpu.make_async_copy(wave_hbm, gathered.at[sector], load_sem.at[0]),
        pltpu.make_async_copy(right_hbm, right, load_sem.at[1]),
        pltpu.make_async_copy(left_hbm.at[0, :, :, mine], left.at[0], load_sem.at[2]),
    ]
    for load in loads:
        load.start()

    barrier = pltpu.get_barrier_semaphore()
    fam_steps = [(dx, dy) for dy in (0, 2) for dx in range(4) if (dx, dy) != (0, 0)]
    greeted = [(dx, dy, 0, False) for dx, dy in fam_steps]
    greeted += [(0, 1, 0, False), (0, -1, 0, False), (0, 0, 1, False), (0, 0, -1, False), (0, 0, 0, True)]
    for where in greeted:
        pl.semaphore_signal(barrier, inc=1, device_id=device(*where), device_id_type=MESH)

    def chunk_rows(h, j):
        return pl.ds(pl.multiple_of((4 * h + lax.rem(x + j, 4)) * CHUNK, CHUNK), CHUNK)

    def chunk_at(dq, dz, h, j):
        q = 1 - yl if dq else yl
        return gathered.at[q * 8 + lax.rem(z + dz + 8, 8), chunk_rows(h, j)]

    pl.semaphore_wait(barrier, len(greeted))

    def arrival(step, link, source, part):
        dx, dy, dz = LINKS[link]
        return pltpu.make_async_remote_copy(
            src_ref=source, dst_ref=part, send_sem=send_sem, recv_sem=recv_sem.at[step, link],
            device_id=device(-dx, -dy, -dz), device_id_type=MESH,
        )

    to_core = pltpu.make_async_remote_copy(
        src_ref=left_hbm.at[0, :, :, others], dst_ref=left.at[1], send_sem=left_send_sem, recv_sem=left_recv_sem,
        device_id=device(0, 0, 0, True), device_id_type=MESH,
    )
    live_slots = counts_ref[f, sector]
    arrives = {parts_of(label): (step, link) for step, row in enumerate(ROUNDS) for link, label in enumerate(row) if label >= 0}

    def wait_for(chunk):
        if chunk in arrives:
            part = chunk_at(*chunk)
            arrival(*arrives.pop(chunk), part, part).wait_recv()

    for step in range(len(ROUNDS)):
        if step == LAG:
            loads[0].wait()
        sends = [(link, sender_parts(link, label)) for link, label in enumerate(ROUNDS[step]) if label >= 0]
        for link, chunk in sorted(sends, key=lambda send: send[1] in arrives):
            wait_for(chunk)
            part = chunk_at(*chunk)
            source = wave_hbm.at[chunk_rows(*chunk[2:])] if chunk[:2] == (0, 0) and step < LAG else part
            arrival(step, link, source, part).start()
        if step == 0:
            to_core.start()
            loads[1].wait()
            right_t[...] = right[0].astype(jnp.float32).T.astype(jnp.bfloat16)
        if step == len(ROUNDS) - 8:
            loads[2].wait()
            to_core.wait_recv()
        k = step - (len(ROUNDS) - 8)
        if 0 <= k < KMAX:
            column = lax.broadcasted_iota(jnp.int32, (1, ROWS), 1)
            used = jnp.where(column + core * ROWS < used_ref[sources_ref[f, k, sector]], 1.0, 0.0)
            used = jnp.where(k + jnp.zeros_like(column) < live_slots, used, 0.0).astype(jnp.bfloat16)
            for side in range(2):
                left[side, k] = left[side, k] * used

    for chunk in sorted(arrives, key=arrives.get):
        wait_for(chunk)

    def product(side, part):
        def add_slot(k, carry):
            a = sources_ref[f, k, sector]
            slot = k + jnp.zeros((DEPTH, COLS), jnp.int32)
            term = jnp.dot(
                left[side, k, part * DEPTH : (part + 1) * DEPTH, :], gathered[a], preferred_element_type=jnp.float32
            )
            sums[...] += jnp.where(slot < live_slots, term, 0.0)
            return carry

        sums[...] = jnp.zeros_like(sums)
        lax.fori_loop(0, KMAX, add_slot, 0, unroll=True)
        return sums[...]

    halves = [
        pltpu.make_async_remote_copy(
            src_ref=half_out.at[part], dst_ref=half_in.at[part], send_sem=half_send_sem.at[part],
            recv_sem=half_recv_sem.at[part], device_id=device(0, 0, 0, True), device_id_type=MESH,
        )
        for part in range(PARTS)
    ]
    def for_other_core(part):
        half_out[part] = product(1, part).astype(jnp.bfloat16)
        halves[part].start()

    def for_families(part):
        own_half = product(0, part)
        halves[part].wait_recv()
        partial_sum = (own_half + half_in[part].astype(jnp.float32)).astype(jnp.bfloat16)
        turned = lax.dot_general(
            right_t[...], partial_sum, (((1,), (1,)), ((), ())), preferred_element_type=jnp.float32
        )
        outgoing[part] = turned.astype(jnp.bfloat16).reshape(FAM, COLS // FAM, DEPTH)
        for dx, dy in fam_steps:
            there = device(dx, dy, 0)
            pltpu.make_async_remote_copy(
                src_ref=outgoing.at[part, there[0]], dst_ref=incoming.at[part, f], send_sem=fam_send_sem,
                recv_sem=fam_recv_sem.at[part], device_id=there, device_id_type=MESH,
            ).start()

    for_other_core(0)
    for part in range(PARTS):
        if part + 1 < PARTS:
            for_other_core(part + 1)
        for_families(part)

    for part in range(PARTS):
        rest = incoming.at[part, pl.ds(0, FAM - 1)]
        pltpu.make_async_copy(rest, rest, fam_recv_sem.at[part]).wait()
        incoming[part, f] = outgoing[part, f]
        total = jnp.sum(incoming[part].astype(jnp.float32), axis=0)
        row = core * ROWS + part * DEPTH + lax.broadcasted_iota(jnp.int32, total.shape, 1)
        out_ref[:, part * DEPTH : (part + 1) * DEPTH] = jnp.where(row < used_ref[sector], total, 0.0).astype(jnp.bfloat16)

    for part in range(PARTS):
        rest = outgoing.at[part, pl.ds(0, FAM - 1)]
        pltpu.make_async_copy(rest, rest, fam_send_sem).wait()
        halves[part].wait_send()
    to_core.wait_send()
    sent = gathered.at[pl.ds(0, S - 1)]
    pltpu.make_async_copy(sent, sent, send_sem).wait()


def body(wavefunction, left_blocks, right_blocks, term_sources, term_counts, sector_rows):
    vmem = pl.BlockSpec(memory_space=pltpu.VMEM)
    smem = pl.BlockSpec(memory_space=pltpu.SMEM)
    anywhere = pl.BlockSpec(memory_space=pl.ANY)
    turned = pl.pallas_call(
        kernel,
        out_shape=jax.ShapeDtypeStruct((COLS // FAM, ROWS), jnp.bfloat16),
        in_specs=[smem, smem, smem, anywhere, anywhere, anywhere],
        out_specs=vmem,
        scratch_shapes=[
            pltpu.VMEM((S, ROWS, COLS), jnp.bfloat16),
            pltpu.VMEM((2, KMAX, ROWS, ROWS), jnp.bfloat16),
            pltpu.VMEM((1, COLS, COLS), jnp.bfloat16),
            pltpu.VMEM((COLS, COLS), jnp.bfloat16),
            pltpu.VMEM((DEPTH, COLS), jnp.float32),
            pltpu.VMEM((PARTS, DEPTH, COLS), jnp.bfloat16),
            pltpu.VMEM((PARTS, DEPTH, COLS), jnp.bfloat16),
            pltpu.VMEM((PARTS, FAM, COLS // FAM, DEPTH), jnp.bfloat16),
            pltpu.VMEM((PARTS, FAM, COLS // FAM, DEPTH), jnp.bfloat16),
            pltpu.SemaphoreType.DMA((3,)),
            pltpu.SemaphoreType.DMA,
            pltpu.SemaphoreType.DMA((len(ROUNDS), len(LINKS))),
            pltpu.SemaphoreType.DMA,
            pltpu.SemaphoreType.DMA,
            pltpu.SemaphoreType.DMA((PARTS,)),
            pltpu.SemaphoreType.DMA((PARTS,)),
            pltpu.SemaphoreType.DMA,
            pltpu.SemaphoreType.DMA((PARTS,)),
        ],
        compiler_params=pltpu.CompilerParams(
            collective_id=0, has_side_effects=True, vmem_limit_bytes=56 * 2**20
        ),
        cost_estimate=pl.CostEstimate(flops=2 * KMAX * ROWS * SROW * COLS, bytes_accessed=9 * 2**20, transcendentals=0),
        name="gather_multiply_scatter",
    )(jnp.swapaxes(term_sources, 1, 2), term_counts, sector_rows, wavefunction, left_blocks, right_blocks)
    return turned.T


def solution(mesh):
    return jax.shard_map(
        body,
        mesh=mesh,
        in_specs=(
            P("owner", None),
            P("fam", None, "owner", None),
            P("fam", None, None),
            P(),
            P(),
            P(),
        ),
        out_specs=P("owner", "fam"),
        check_vma=False,
    )
```

```python
import functools

import jax
import jax.numpy as jnp
from jax import lax
from jax.experimental import pallas as pl
from jax.experimental.pallas import tpu as pltpu
from jax.sharding import PartitionSpec as P

MESH = pl.DeviceIdType.MESH
S, SROW, COLS, KMAX, FAM = 16, 1024, 512, 8, 8
ROWS = 512
CHUNK = ROWS // 4
WIDTH = COLS // 2
LAG = 3
PARTS = 4
MASK_AT, FIRST_AT = 9, 18
DEPTH = ROWS // PARTS
LINKS = ((0, 0, 1), (0, 0, -1), (0, 1, 0), (0, -1, 0), (1, 0, 0), (-1, 0, 0))

ROUNDS = (
    (36, 18, 88, 89, -1, -1),
    (35, 22, 95, 92, -1, -1),
    (32, 19, 90, 93, -1, -1),
    (97, 10, 82, 100, 37, 39),
    (43, 80, 99, 91, 23, 34),
    (98, 81, 96, 83, 16, 17),
    (105, 20, 33, 74, 11, 9),
    (51, 15, 101, 103, 40, 42),
    (104, 8, 87, 107, 94, 38),
    (113, 3, 73, 41, 106, 21),
    (109, 66, 115, 75, 48, 50),
    (59, 0, 79, 72, 102, 86),
    (121, 13, 49, 67, 114, 2),
    (56, 7, 85, 112, 110, 65),
    (117, 122, 64, 123, 76, 58),
    (44, 5, 77, 57, 1, 120),
    (118, 63, 71, 45, 111, 78),
    (47, 68, 53, 46, 84, 116),
    (108, 61, 69, 12, 6, 4),
    (126, 55, 54, 14, 119, 62),
    (125, 124, 52, 127, 60, 70),
)


def parts_of(label):
    return label // 64, label // 8 % 8 - 3, label // 4 % 2, label % 4


def sender_parts(link, label):
    dq, dz, h, j = parts_of(label)
    dx, dy, step = LINKS[link]
    return (dq + dy) % 2, (dz - step + 3) % 8 - 3, h, (j - dx) % 4


def kernel(
    sources_ref,
    counts_ref,
    used_ref,
    wave_hbm,
    left_hbm,
    right_hbm,
    out_ref,
    gathered_first,
    gathered_second,
    left,
    right,
    right_t,
    sums,
    first,
    half_out,
    half_in,
    outgoing,
    incoming,
    load_sem,
    send_sem,
    recv_sem,
    left_send_sem,
    left_recv_sem,
    half_send_sem,
    half_recv_sem,
    fam_send_sem,
    fam_recv_sem,
):
    gathered = (gathered_first, gathered_second)
    f = lax.axis_index("fam")
    o = lax.axis_index("owner")
    x, yh = lax.rem(f, 4), f // 4
    core, z, yl = lax.rem(o, 2), lax.rem(o // 2, 8), o // 16
    y = yh * 2 + yl
    sector = o // 2

    def device(dx, dy, dz, other=False):
        nx, ny, nz = lax.rem(x + dx + 4, 4), lax.rem(y + dy + 4, 4), lax.rem(z + dz + 8, 8)
        c = 1 - core if other else core
        return ((ny // 2) * 4 + nx, (lax.rem(ny, 2) * 8 + nz) * 2 + c)

    mine = pl.ds(pl.multiple_of(core * ROWS, ROWS), ROWS)
    others = pl.ds(pl.multiple_of((1 - core) * ROWS, ROWS), ROWS)
    loads = [
        pltpu.make_async_copy(wave_hbm.at[:, pl.ds(h * WIDTH, WIDTH)], gathered[h].at[sector], load_sem.at[h])
        for h in range(2)
    ] + [
        pltpu.make_async_copy(right_hbm, right, load_sem.at[3]),
        pltpu.make_async_copy(left_hbm.at[0, :, :, mine], left.at[0], load_sem.at[2]),
    ]
    for load in loads:
        load.start()

    barrier = pltpu.get_barrier_semaphore()
    fam_steps = [(dx, dy) for dy in (0, 2) for dx in range(4) if (dx, dy) != (0, 0)]
    greeted = [(1, 0, 0, False), (-1, 0, 0, False)]
    greeted += [(0, 1, 0, False), (0, -1, 0, False), (0, 0, 1, False), (0, 0, -1, False), (0, 0, 0, True)]
    for where in greeted:
        pl.semaphore_signal(barrier, inc=1, device_id=device(*where), device_id_type=MESH)

    def chunk_rows(j):
        return pl.ds(pl.multiple_of(lax.rem(x + j, 4) * CHUNK, CHUNK), CHUNK)

    def chunk_at(dq, dz, h, j):
        q = 1 - yl if dq else yl
        return gathered[h].at[q * 8 + lax.rem(z + dz + 8, 8), chunk_rows(j)]

    pl.semaphore_wait(barrier, len(greeted))

    def arrival(step, link, source, part):
        dx, dy, dz = LINKS[link]
        return pltpu.make_async_remote_copy(
            src_ref=source, dst_ref=part, send_sem=send_sem, recv_sem=recv_sem.at[step, link],
            device_id=device(-dx, -dy, -dz), device_id_type=MESH,
        )

    to_core = pltpu.make_async_remote_copy(
        src_ref=left_hbm.at[0, :, :, others], dst_ref=left.at[1], send_sem=left_send_sem, recv_sem=left_recv_sem,
        device_id=device(0, 0, 0, True), device_id_type=MESH,
    )
    live_slots = counts_ref[f, sector]

    def product(side, h, start, count):
        def add_slot(k, carry):
            a = sources_ref[f, k, sector]
            slot = k + jnp.zeros((count, WIDTH), jnp.int32)
            term = jnp.dot(left[side, k, start : start + count, :], gathered[h][a], preferred_element_type=jnp.float32)
            sums[:count] += jnp.where(slot < live_slots, term, 0.0)
            return carry

        sums[:count] = jnp.zeros((count, WIDTH), jnp.float32)
        lax.fori_loop(0, KMAX, add_slot, 0, unroll=True)
        return sums[:count]

    def times_right(h, partial_sum):
        return lax.dot_general(
            right_t[:, h * WIDTH : (h + 1) * WIDTH], partial_sum.astype(jnp.bfloat16), (((1,), (1,)), ((), ())),
            preferred_element_type=jnp.float32,
        )

    def half_copy(i, h, rows):
        return pltpu.make_async_remote_copy(
            src_ref=half_out.at[h, rows], dst_ref=half_in.at[h, rows], send_sem=half_send_sem.at[i],
            recv_sem=half_recv_sem.at[i], device_id=device(0, 0, 0, True), device_id_type=MESH,
        )

    halves = [half_copy(0, 0, pl.ds(0, ROWS))]
    halves += [half_copy(1 + part, 1, pl.ds(part * DEPTH, DEPTH)) for part in range(PARTS)]

    arrives = {parts_of(label): (step, link) for step, row in enumerate(ROUNDS) for link, label in enumerate(row) if label >= 0}

    def wait_for(chunk):
        if chunk in arrives:
            part = chunk_at(*chunk)
            arrival(*arrives.pop(chunk), part, part).wait_recv()

    for step in range(len(ROUNDS)):
        if step == LAG:
            loads[0].wait()
            loads[1].wait()
        sends = [(link, sender_parts(link, label)) for link, label in enumerate(ROUNDS[step]) if label >= 0]
        for link, chunk in sorted(sends, key=lambda send: send[1] in arrives):
            wait_for(chunk)
            part = chunk_at(*chunk)
            source = part
            if chunk[:2] == (0, 0) and step < LAG:
                source = wave_hbm.at[chunk_rows(chunk[3]), pl.ds(chunk[2] * WIDTH, WIDTH)]
            arrival(step, link, source, part).start()
        if step == 0:
            to_core.start()
            loads[2].wait()
            right_t[...] = right[0].astype(jnp.float32).T.astype(jnp.bfloat16)
        if step == MASK_AT:
            loads[3].wait()
            to_core.wait_recv()
        k = step - MASK_AT
        if 0 <= k < KMAX:
            column = core * ROWS + lax.broadcasted_iota(jnp.int32, (1, ROWS), 1)
            used = jnp.where(column < used_ref[sources_ref[f, k, sector]], 1.0, 0.0).astype(jnp.bfloat16)
            for side in range(2):
                left[side, k] = left[side, k] * used
        if step == FIRST_AT:
            for chunk in sorted(arrives, key=arrives.get):
                if chunk[2] == 0:
                    wait_for(chunk)
            half_out[0] = product(1, 0, 0, ROWS).astype(jnp.bfloat16)
            halves[0].start()
        if step == FIRST_AT + 1:
            product(0, 0, 0, ROWS)
        if step == FIRST_AT + 2:
            halves[0].wait_recv()
            first[...] = times_right(0, sums[...] + half_in[0].astype(jnp.float32))
    for chunk in sorted(arrives, key=arrives.get):
        wait_for(chunk)

    for part in range(PARTS):
        half_out[1, part * DEPTH : (part + 1) * DEPTH] = product(1, 1, part * DEPTH, DEPTH).astype(jnp.bfloat16)
        halves[1 + part].start()
    for part in range(PARTS):
        rows = slice(part * DEPTH, (part + 1) * DEPTH)
        own_half = product(0, 1, part * DEPTH, DEPTH)
        halves[1 + part].wait_recv()
        turned = first[:, rows] + times_right(1, own_half + half_in[1, rows].astype(jnp.float32))
        outgoing[part] = turned.astype(jnp.bfloat16).reshape(FAM, COLS // FAM, DEPTH)
        for dx, dy in fam_steps:
            there = device(dx, dy, 0)
            pltpu.make_async_remote_copy(
                src_ref=outgoing.at[part, there[0]], dst_ref=incoming.at[part, f], send_sem=fam_send_sem,
                recv_sem=fam_recv_sem.at[part], device_id=there, device_id_type=MESH,
            ).start()

    for part in range(PARTS):
        rest = incoming.at[part, pl.ds(0, FAM - 1)]
        pltpu.make_async_copy(rest, rest, fam_recv_sem.at[part]).wait()
        incoming[part, f] = outgoing[part, f]
        total = jnp.sum(incoming[part].astype(jnp.float32), axis=0)
        row = core * ROWS + part * DEPTH + lax.broadcasted_iota(jnp.int32, total.shape, 1)
        out_ref[:, part * DEPTH : (part + 1) * DEPTH] = jnp.where(row < used_ref[sector], total, 0.0).astype(jnp.bfloat16)

    for part in range(PARTS):
        rest = outgoing.at[part, pl.ds(0, FAM - 1)]
        pltpu.make_async_copy(rest, rest, fam_send_sem).wait()
    for half in halves:
        half.wait_send()
    to_core.wait_send()
    for half in gathered:
        sent = half.at[pl.ds(0, S - 1)]
        pltpu.make_async_copy(sent, sent, send_sem).wait()


def body(wavefunction, left_blocks, right_blocks, term_sources, term_counts, sector_rows):
    vmem = pl.BlockSpec(memory_space=pltpu.VMEM)
    smem = pl.BlockSpec(memory_space=pltpu.SMEM)
    anywhere = pl.BlockSpec(memory_space=pl.ANY)
    turned = pl.pallas_call(
        kernel,
        out_shape=jax.ShapeDtypeStruct((COLS // FAM, ROWS), jnp.bfloat16),
        in_specs=[smem, smem, smem, anywhere, anywhere, anywhere],
        out_specs=vmem,
        scratch_shapes=[
            pltpu.VMEM((S, ROWS, WIDTH), jnp.bfloat16),
            pltpu.VMEM((S, ROWS, WIDTH), jnp.bfloat16),
            pltpu.VMEM((2, KMAX, ROWS, ROWS), jnp.bfloat16),
            pltpu.VMEM((1, COLS, COLS), jnp.bfloat16),
            pltpu.VMEM((COLS, COLS), jnp.bfloat16),
            pltpu.VMEM((ROWS, WIDTH), jnp.float32),
            pltpu.VMEM((COLS, ROWS), jnp.float32),
            pltpu.VMEM((2, ROWS, WIDTH), jnp.bfloat16),
            pltpu.VMEM((2, ROWS, WIDTH), jnp.bfloat16),
            pltpu.VMEM((PARTS, FAM, COLS // FAM, DEPTH), jnp.bfloat16),
            pltpu.VMEM((PARTS, FAM, COLS // FAM, DEPTH), jnp.bfloat16),
            pltpu.SemaphoreType.DMA((4,)),
            pltpu.SemaphoreType.DMA,
            pltpu.SemaphoreType.DMA((len(ROUNDS), len(LINKS))),
            pltpu.SemaphoreType.DMA,
            pltpu.SemaphoreType.DMA,
            pltpu.SemaphoreType.DMA((1 + PARTS,)),
            pltpu.SemaphoreType.DMA((1 + PARTS,)),
            pltpu.SemaphoreType.DMA,
            pltpu.SemaphoreType.DMA((PARTS,)),
        ],
        compiler_params=pltpu.CompilerParams(
            collective_id=0, has_side_effects=True, vmem_limit_bytes=56 * 2**20
        ),
        cost_estimate=pl.CostEstimate(flops=2 * KMAX * ROWS * SROW * COLS, bytes_accessed=9 * 2**20, transcendentals=0),
        name="gather_multiply_scatter",
    )(jnp.swapaxes(term_sources, 1, 2), term_counts, sector_rows, wavefunction, left_blocks, right_blocks)
    return turned.T


def solution(mesh):
    return jax.shard_map(
        body,
        mesh=mesh,
        in_specs=(
            P("owner", None),
            P("fam", None, "owner", None),
            P("fam", None, None),
            P(),
            P(),
            P(),
        ),
        out_specs=P("owner", "fam"),
        check_vma=False,
    )
```

```python
import functools

import jax
import jax.numpy as jnp
from jax import lax
from jax.experimental import pallas as pl
from jax.experimental.pallas import tpu as pltpu
from jax.sharding import PartitionSpec as P

MESH = pl.DeviceIdType.MESH
S, SROW, COLS, KMAX, FAM = 16, 1024, 512, 8, 8
ROWS = 512
CHUNK = ROWS // 4
WIDTH = COLS // 2
LAG = 3
PARTS = 4
MASK_AT, FIRST_AT = 9, 18
DEPTH = ROWS // PARTS
LINKS = ((0, 0, 1), (0, 0, -1), (0, 1, 0), (0, -1, 0), (1, 0, 0), (-1, 0, 0))

ROUNDS = (
    (36, 18, 88, 89, -1, -1),
    (35, 22, 95, 92, -1, -1),
    (32, 19, 90, 93, -1, -1),
    (97, 10, 82, 100, 37, 39),
    (43, 80, 99, 91, 23, 34),
    (98, 81, 96, 83, 16, 17),
    (105, 20, 33, 74, 11, 9),
    (51, 15, 101, 103, 40, 42),
    (104, 8, 87, 107, 94, 38),
    (113, 3, 73, 41, 106, 21),
    (109, 66, 115, 75, 48, 50),
    (59, 0, 79, 72, 102, 86),
    (121, 13, 49, 67, 114, 2),
    (56, 7, 85, 112, 110, 65),
    (117, 122, 64, 123, 76, 58),
    (44, 5, 77, 57, 1, 120),
    (118, 63, 71, 45, 111, 78),
    (47, 68, 53, 46, 84, 116),
    (108, 61, 69, 12, 6, 4),
    (126, 55, 54, 14, 119, 62),
    (125, 124, 52, 127, 60, 70),
)


def parts_of(label):
    return label // 64, label // 8 % 8 - 3, label // 4 % 2, label % 4


def sender_parts(link, label):
    dq, dz, h, j = parts_of(label)
    dx, dy, step = LINKS[link]
    return (dq + dy) % 2, (dz - step + 3) % 8 - 3, h, (j - dx) % 4


def kernel(
    sources_ref,
    counts_ref,
    used_ref,
    wave_hbm,
    left_hbm,
    right_hbm,
    out_ref,
    gathered_first,
    gathered_second,
    left,
    right,
    right_t,
    sums,
    first,
    half_out,
    half_in,
    outgoing,
    incoming,
    load_sem,
    send_sem,
    recv_sem,
    left_send_sem,
    left_recv_sem,
    half_send_sem,
    half_recv_sem,
    fam_send_sem,
    fam_recv_sem,
):
    gathered = (gathered_first, gathered_second)
    f = lax.axis_index("fam")
    o = lax.axis_index("owner")
    x, yh = lax.rem(f, 4), f // 4
    core, z, yl = lax.rem(o, 2), lax.rem(o // 2, 8), o // 16
    y = yh * 2 + yl
    sector = o // 2

    def device(dx, dy, dz, other=False):
        nx, ny, nz = lax.rem(x + dx + 4, 4), lax.rem(y + dy + 4, 4), lax.rem(z + dz + 8, 8)
        c = 1 - core if other else core
        return ((ny // 2) * 4 + nx, (lax.rem(ny, 2) * 8 + nz) * 2 + c)

    mine = pl.ds(pl.multiple_of(core * ROWS, ROWS), ROWS)
    others = pl.ds(pl.multiple_of((1 - core) * ROWS, ROWS), ROWS)
    loads = [
        pltpu.make_async_copy(wave_hbm.at[:, pl.ds(h * WIDTH, WIDTH)], gathered[h].at[sector], load_sem.at[h])
        for h in range(2)
    ] + [
        pltpu.make_async_copy(right_hbm, right, load_sem.at[3]),
        pltpu.make_async_copy(left_hbm.at[0, :, :, mine], left.at[0], load_sem.at[2]),
    ]
    for load in loads:
        load.start()

    barrier = pltpu.get_barrier_semaphore()
    fam_steps = [(2, 2), (1, 2), (3, 2), (0, 2), (2, 0), (1, 0), (3, 0)]
    greeted = [(1, 0, 0, False), (-1, 0, 0, False)]
    greeted += [(0, 1, 0, False), (0, -1, 0, False), (0, 0, 1, False), (0, 0, -1, False), (0, 0, 0, True)]
    for where in greeted:
        pl.semaphore_signal(barrier, inc=1, device_id=device(*where), device_id_type=MESH)

    def chunk_rows(j):
        return pl.ds(pl.multiple_of(lax.rem(x + j, 4) * CHUNK, CHUNK), CHUNK)

    def chunk_at(dq, dz, h, j):
        q = 1 - yl if dq else yl
        return gathered[h].at[q * 8 + lax.rem(z + dz + 8, 8), chunk_rows(j)]

    pl.semaphore_wait(barrier, len(greeted))

    def arrival(step, link, source, part):
        dx, dy, dz = LINKS[link]
        return pltpu.make_async_remote_copy(
            src_ref=source, dst_ref=part, send_sem=send_sem, recv_sem=recv_sem.at[step, link],
            device_id=device(-dx, -dy, -dz), device_id_type=MESH,
        )

    to_core = pltpu.make_async_remote_copy(
        src_ref=left_hbm.at[0, :, :, others], dst_ref=left.at[1], send_sem=left_send_sem, recv_sem=left_recv_sem,
        device_id=device(0, 0, 0, True), device_id_type=MESH,
    )
    live_slots = counts_ref[f, sector]

    def product(side, h, start, count):
        def add_slot(k, carry):
            a = sources_ref[f, k, sector]
            slot = k + jnp.zeros((count, WIDTH), jnp.int32)
            term = jnp.dot(left[side, k, start : start + count, :], gathered[h][a], preferred_element_type=jnp.float32)
            sums[:count] += jnp.where(slot < live_slots, term, 0.0)
            return carry

        sums[:count] = jnp.zeros((count, WIDTH), jnp.float32)
        lax.fori_loop(0, KMAX, add_slot, 0, unroll=True)
        return sums[:count]

    def times_right(h, partial_sum):
        return lax.dot_general(
            right_t[:, h * WIDTH : (h + 1) * WIDTH], partial_sum.astype(jnp.bfloat16), (((1,), (1,)), ((), ())),
            preferred_element_type=jnp.float32,
        )

    def half_copy(i, h, rows):
        return pltpu.make_async_remote_copy(
            src_ref=half_out.at[h, rows], dst_ref=half_in.at[h, rows], send_sem=half_send_sem.at[i],
            recv_sem=half_recv_sem.at[i], device_id=device(0, 0, 0, True), device_id_type=MESH,
        )

    halves = [half_copy(0, 0, pl.ds(0, ROWS))]
    halves += [half_copy(1 + part, 1, pl.ds(part * DEPTH, DEPTH)) for part in range(PARTS)]

    arrives = {parts_of(label): (step, link) for step, row in enumerate(ROUNDS) for link, label in enumerate(row) if label >= 0}

    def wait_for(chunk):
        if chunk in arrives:
            part = chunk_at(*chunk)
            arrival(*arrives.pop(chunk), part, part).wait_recv()

    for step in range(len(ROUNDS)):
        if step == LAG:
            loads[0].wait()
            loads[1].wait()
        sends = [(link, sender_parts(link, label)) for link, label in enumerate(ROUNDS[step]) if label >= 0]
        for link, chunk in sorted(sends, key=lambda send: send[1] in arrives):
            wait_for(chunk)
            part = chunk_at(*chunk)
            source = part
            if chunk[:2] == (0, 0) and step < LAG:
                source = wave_hbm.at[chunk_rows(chunk[3]), pl.ds(chunk[2] * WIDTH, WIDTH)]
            arrival(step, link, source, part).start()
        if step == 0:
            to_core.start()
            loads[2].wait()
            right_t[...] = right[0].astype(jnp.float32).T.astype(jnp.bfloat16)
        if step == MASK_AT:
            loads[3].wait()
            to_core.wait_recv()
        k = step - MASK_AT
        if 0 <= k < KMAX:
            column = core * ROWS + lax.broadcasted_iota(jnp.int32, (1, ROWS), 1)
            used = jnp.where(column < used_ref[sources_ref[f, k, sector]], 1.0, 0.0).astype(jnp.bfloat16)
            for side in range(2):
                left[side, k] = left[side, k] * used
        if step == FIRST_AT:
            for chunk in sorted(arrives, key=arrives.get):
                if chunk[2] == 0:
                    wait_for(chunk)
            half_out[0] = product(1, 0, 0, ROWS).astype(jnp.bfloat16)
            halves[0].start()
        if step == FIRST_AT + 1:
            product(0, 0, 0, ROWS)
        if step == FIRST_AT + 2:
            halves[0].wait_recv()
            first[...] = times_right(0, sums[...] + half_in[0].astype(jnp.float32))
    for chunk in sorted(arrives, key=arrives.get):
        wait_for(chunk)

    for part in range(PARTS):
        half_out[1, part * DEPTH : (part + 1) * DEPTH] = product(1, 1, part * DEPTH, DEPTH).astype(jnp.bfloat16)
        halves[1 + part].start()
    for part in range(PARTS):
        rows = slice(part * DEPTH, (part + 1) * DEPTH)
        own_half = product(0, 1, part * DEPTH, DEPTH)
        halves[1 + part].wait_recv()
        turned = first[:, rows] + times_right(1, own_half + half_in[1, rows].astype(jnp.float32))
        outgoing[part] = turned.astype(jnp.bfloat16).reshape(FAM, COLS // FAM, DEPTH)
        for dx, dy in fam_steps:
            there = device(dx, dy, 0)
            pltpu.make_async_remote_copy(
                src_ref=outgoing.at[part, there[0]], dst_ref=incoming.at[part, f], send_sem=fam_send_sem,
                recv_sem=fam_recv_sem.at[part], device_id=there, device_id_type=MESH,
            ).start()

    for part in range(PARTS):
        rest = incoming.at[part, pl.ds(0, FAM - 1)]
        pltpu.make_async_copy(rest, rest, fam_recv_sem.at[part]).wait()
        incoming[part, f] = outgoing[part, f]
        total = jnp.sum(incoming[part].astype(jnp.float32), axis=0)
        row = core * ROWS + part * DEPTH + lax.broadcasted_iota(jnp.int32, total.shape, 1)
        out_ref[:, part * DEPTH : (part + 1) * DEPTH] = jnp.where(row < used_ref[sector], total, 0.0).astype(jnp.bfloat16)

    for part in range(PARTS):
        rest = outgoing.at[part, pl.ds(0, FAM - 1)]
        pltpu.make_async_copy(rest, rest, fam_send_sem).wait()
    for half in halves:
        half.wait_send()
    to_core.wait_send()
    for half in gathered:
        sent = half.at[pl.ds(0, S - 1)]
        pltpu.make_async_copy(sent, sent, send_sem).wait()


def body(wavefunction, left_blocks, right_blocks, term_sources, term_counts, sector_rows):
    vmem = pl.BlockSpec(memory_space=pltpu.VMEM)
    smem = pl.BlockSpec(memory_space=pltpu.SMEM)
    anywhere = pl.BlockSpec(memory_space=pl.ANY)
    turned = pl.pallas_call(
        kernel,
        out_shape=jax.ShapeDtypeStruct((COLS // FAM, ROWS), jnp.bfloat16),
        in_specs=[smem, smem, smem, anywhere, anywhere, anywhere],
        out_specs=vmem,
        scratch_shapes=[
            pltpu.VMEM((S, ROWS, WIDTH), jnp.bfloat16),
            pltpu.VMEM((S, ROWS, WIDTH), jnp.bfloat16),
            pltpu.VMEM((2, KMAX, ROWS, ROWS), jnp.bfloat16),
            pltpu.VMEM((1, COLS, COLS), jnp.bfloat16),
            pltpu.VMEM((COLS, COLS), jnp.bfloat16),
            pltpu.VMEM((ROWS, WIDTH), jnp.float32),
            pltpu.VMEM((COLS, ROWS), jnp.float32),
            pltpu.VMEM((2, ROWS, WIDTH), jnp.bfloat16),
            pltpu.VMEM((2, ROWS, WIDTH), jnp.bfloat16),
            pltpu.VMEM((PARTS, FAM, COLS // FAM, DEPTH), jnp.bfloat16),
            pltpu.VMEM((PARTS, FAM, COLS // FAM, DEPTH), jnp.bfloat16),
            pltpu.SemaphoreType.DMA((4,)),
            pltpu.SemaphoreType.DMA,
            pltpu.SemaphoreType.DMA((len(ROUNDS), len(LINKS))),
            pltpu.SemaphoreType.DMA,
            pltpu.SemaphoreType.DMA,
            pltpu.SemaphoreType.DMA((1 + PARTS,)),
            pltpu.SemaphoreType.DMA((1 + PARTS,)),
            pltpu.SemaphoreType.DMA,
            pltpu.SemaphoreType.DMA((PARTS,)),
        ],
        compiler_params=pltpu.CompilerParams(
            collective_id=0, has_side_effects=True, vmem_limit_bytes=56 * 2**20
        ),
        cost_estimate=pl.CostEstimate(flops=2 * KMAX * ROWS * SROW * COLS, bytes_accessed=9 * 2**20, transcendentals=0),
        name="gather_multiply_scatter",
    )(jnp.swapaxes(term_sources, 1, 2), term_counts, sector_rows, wavefunction, left_blocks, right_blocks)
    return turned.T


def solution(mesh):
    return jax.shard_map(
        body,
        mesh=mesh,
        in_specs=(
            P("owner", None),
            P("fam", None, "owner", None),
            P("fam", None, None),
            P(),
            P(),
            P(),
        ),
        out_specs=P("owner", "fam"),
        check_vma=False,
    )
```

```python
import functools

import jax
import jax.numpy as jnp
from jax import lax
from jax.experimental import pallas as pl
from jax.experimental.pallas import tpu as pltpu
from jax.sharding import PartitionSpec as P

MESH = pl.DeviceIdType.MESH
S, SROW, COLS, KMAX, FAM = 16, 1024, 512, 8, 8
ROWS = 512
CHUNK = ROWS // 4
WIDTH = COLS // 2
LAG = 3
PARTS = 4
MASK_AT, FIRST_AT = 9, 18
DEPTH = ROWS // PARTS
LINKS = ((0, 0, 1), (0, 0, -1), (0, 1, 0), (0, -1, 0), (1, 0, 0), (-1, 0, 0))

ROUNDS = (
    (36, 18, 88, 89, -1, -1),
    (35, 22, 95, 92, -1, -1),
    (32, 19, 90, 93, -1, -1),
    (97, 10, 82, 100, 37, 39),
    (43, 80, 99, 91, 23, 34),
    (98, 81, 96, 83, 16, 17),
    (105, 20, 33, 74, 11, 9),
    (51, 15, 101, 103, 40, 42),
    (104, 8, 87, 107, 94, 38),
    (113, 3, 73, 41, 106, 21),
    (109, 66, 115, 75, 48, 50),
    (59, 0, 79, 72, 102, 86),
    (121, 13, 49, 67, 114, 2),
    (56, 7, 85, 112, 110, 65),
    (117, 122, 64, 123, 76, 58),
    (44, 5, 77, 57, 1, 120),
    (118, 63, 71, 45, 111, 78),
    (47, 68, 53, 46, 84, 116),
    (108, 61, 69, 12, 6, 4),
    (126, 55, 54, 14, 119, 62),
    (125, 124, 52, 127, 60, 70),
)


def parts_of(label):
    return label // 64, label // 8 % 8 - 3, label // 4 % 2, label % 4


def sender_parts(link, label):
    dq, dz, h, j = parts_of(label)
    dx, dy, step = LINKS[link]
    return (dq + dy) % 2, (dz - step + 3) % 8 - 3, h, (j - dx) % 4


def kernel(
    sources_ref,
    counts_ref,
    used_ref,
    wave_hbm,
    left_hbm,
    right_hbm,
    out_ref,
    gathered_first,
    gathered_second,
    left,
    right,
    right_t,
    sums,
    first,
    half_out,
    half_in,
    outgoing,
    incoming,
    load_sem,
    send_sem,
    recv_sem,
    left_send_sem,
    left_recv_sem,
    half_send_sem,
    half_recv_sem,
    fam_send_sem,
    fam_recv_sem,
):
    gathered = (gathered_first, gathered_second)
    f = lax.axis_index("fam")
    o = lax.axis_index("owner")
    x, yh = lax.rem(f, 4), f // 4
    core, z, yl = lax.rem(o, 2), lax.rem(o // 2, 8), o // 16
    y = yh * 2 + yl
    sector = o // 2

    def device(dx, dy, dz, other=False):
        nx, ny, nz = lax.rem(x + dx + 4, 4), lax.rem(y + dy + 4, 4), lax.rem(z + dz + 8, 8)
        c = 1 - core if other else core
        return ((ny // 2) * 4 + nx, (lax.rem(ny, 2) * 8 + nz) * 2 + c)

    mine = pl.ds(pl.multiple_of(core * ROWS, ROWS), ROWS)
    others = pl.ds(pl.multiple_of((1 - core) * ROWS, ROWS), ROWS)
    loads = [
        pltpu.make_async_copy(wave_hbm.at[:, pl.ds(h * WIDTH, WIDTH)], gathered[h].at[sector], load_sem.at[h])
        for h in range(2)
    ] + [
        pltpu.make_async_copy(right_hbm, right, load_sem.at[3]),
        pltpu.make_async_copy(left_hbm.at[0, :, :, mine], left.at[0], load_sem.at[2]),
    ]
    barrier = pltpu.get_barrier_semaphore()
    fam_steps = [(2, 2), (1, 2), (3, 2), (0, 2), (2, 0), (1, 0), (3, 0)]
    greeted = [(1, 0, 0, False), (-1, 0, 0, False)]
    greeted += [(0, 1, 0, False), (0, -1, 0, False), (0, 0, 1, False), (0, 0, -1, False), (0, 0, 0, True)]
    for where in greeted:
        pl.semaphore_signal(barrier, inc=1, device_id=device(*where), device_id_type=MESH)
    for load in loads:
        load.start()

    def chunk_rows(j):
        return pl.ds(pl.multiple_of(lax.rem(x + j, 4) * CHUNK, CHUNK), CHUNK)

    def chunk_at(dq, dz, h, j):
        q = 1 - yl if dq else yl
        return gathered[h].at[q * 8 + lax.rem(z + dz + 8, 8), chunk_rows(j)]

    pl.semaphore_wait(barrier, len(greeted))

    def arrival(step, link, source, part):
        dx, dy, dz = LINKS[link]
        return pltpu.make_async_remote_copy(
            src_ref=source, dst_ref=part, send_sem=send_sem, recv_sem=recv_sem.at[step, link],
            device_id=device(-dx, -dy, -dz), device_id_type=MESH,
        )

    to_core = pltpu.make_async_remote_copy(
        src_ref=left_hbm.at[0, :, :, others], dst_ref=left.at[1], send_sem=left_send_sem, recv_sem=left_recv_sem,
        device_id=device(0, 0, 0, True), device_id_type=MESH,
    )
    live_slots = counts_ref[f, sector]

    def product(side, h, start, count):
        def add_slot(k, carry):
            a = sources_ref[f, k, sector]
            slot = k + jnp.zeros((count, WIDTH), jnp.int32)
            term = jnp.dot(left[side, k, start : start + count, :], gathered[h][a], preferred_element_type=jnp.float32)
            sums[:count] += jnp.where(slot < live_slots, term, 0.0)
            return carry

        sums[:count] = jnp.zeros((count, WIDTH), jnp.float32)
        lax.fori_loop(0, KMAX, add_slot, 0, unroll=True)
        return sums[:count]

    def times_right(h, partial_sum):
        return lax.dot_general(
            right_t[:, h * WIDTH : (h + 1) * WIDTH], partial_sum.astype(jnp.bfloat16), (((1,), (1,)), ((), ())),
            preferred_element_type=jnp.float32,
        )

    def half_copy(i, h, rows):
        return pltpu.make_async_remote_copy(
            src_ref=half_out.at[h, rows], dst_ref=half_in.at[h, rows], send_sem=half_send_sem.at[i],
            recv_sem=half_recv_sem.at[i], device_id=device(0, 0, 0, True), device_id_type=MESH,
        )

    halves = [half_copy(0, 0, pl.ds(0, ROWS))]
    halves += [half_copy(1 + part, 1, pl.ds(part * DEPTH, DEPTH)) for part in range(PARTS)]

    arrives = {parts_of(label): (step, link) for step, row in enumerate(ROUNDS) for link, label in enumerate(row) if label >= 0}

    def wait_for(chunk):
        if chunk in arrives:
            part = chunk_at(*chunk)
            arrival(*arrives.pop(chunk), part, part).wait_recv()

    for step in range(len(ROUNDS)):
        if step == LAG:
            loads[0].wait()
            loads[1].wait()
        sends = [(link, sender_parts(link, label)) for link, label in enumerate(ROUNDS[step]) if label >= 0]
        for link, chunk in sorted(sends, key=lambda send: send[1] in arrives):
            wait_for(chunk)
            part = chunk_at(*chunk)
            source = part
            if chunk[:2] == (0, 0) and step < LAG:
                source = wave_hbm.at[chunk_rows(chunk[3]), pl.ds(chunk[2] * WIDTH, WIDTH)]
            arrival(step, link, source, part).start()
        if step == 0:
            to_core.start()
            loads[2].wait()
            right_t[...] = right[0].astype(jnp.float32).T.astype(jnp.bfloat16)
        if step == MASK_AT:
            loads[3].wait()
            to_core.wait_recv()
        k = step - MASK_AT
        if 0 <= k < KMAX:
            column = core * ROWS + lax.broadcasted_iota(jnp.int32, (1, ROWS), 1)
            used = jnp.where(column < used_ref[sources_ref[f, k, sector]], 1.0, 0.0).astype(jnp.bfloat16)
            for side in range(2):
                left[side, k] = left[side, k] * used
        if step == FIRST_AT:
            for chunk in sorted(arrives, key=arrives.get):
                if chunk[2] == 0:
                    wait_for(chunk)
            half_out[0] = product(1, 0, 0, ROWS).astype(jnp.bfloat16)
            halves[0].start()
        if step == FIRST_AT + 1:
            product(0, 0, 0, ROWS)
        if step == FIRST_AT + 2:
            halves[0].wait_recv()
            first[...] = times_right(0, sums[...] + half_in[0].astype(jnp.float32))
    for chunk in sorted(arrives, key=arrives.get):
        wait_for(chunk)

    for part in range(PARTS):
        half_out[1, part * DEPTH : (part + 1) * DEPTH] = product(1, 1, part * DEPTH, DEPTH).astype(jnp.bfloat16)
        halves[1 + part].start()
    for part in range(PARTS):
        rows = slice(part * DEPTH, (part + 1) * DEPTH)
        own_half = product(0, 1, part * DEPTH, DEPTH)
        halves[1 + part].wait_recv()
        turned = first[:, rows] + times_right(1, own_half + half_in[1, rows].astype(jnp.float32))
        outgoing[part] = turned.astype(jnp.bfloat16).reshape(FAM, COLS // FAM, DEPTH)
        for dx, dy in fam_steps:
            there = device(dx, dy, 0)
            pltpu.make_async_remote_copy(
                src_ref=outgoing.at[part, there[0]], dst_ref=incoming.at[part, f], send_sem=fam_send_sem,
                recv_sem=fam_recv_sem.at[part], device_id=there, device_id_type=MESH,
            ).start()

    for part in range(PARTS):
        rest = incoming.at[part, pl.ds(0, FAM - 1)]
        pltpu.make_async_copy(rest, rest, fam_recv_sem.at[part]).wait()
        incoming[part, f] = outgoing[part, f]
        total = jnp.sum(incoming[part].astype(jnp.float32), axis=0)
        row = core * ROWS + part * DEPTH + lax.broadcasted_iota(jnp.int32, total.shape, 1)
        out_ref[:, part * DEPTH : (part + 1) * DEPTH] = jnp.where(row < used_ref[sector], total, 0.0).astype(jnp.bfloat16)

    for part in range(PARTS):
        rest = outgoing.at[part, pl.ds(0, FAM - 1)]
        pltpu.make_async_copy(rest, rest, fam_send_sem).wait()
    for half in halves:
        half.wait_send()
    to_core.wait_send()
    for half in gathered:
        sent = half.at[pl.ds(0, S - 1)]
        pltpu.make_async_copy(sent, sent, send_sem).wait()


def body(wavefunction, left_blocks, right_blocks, term_sources, term_counts, sector_rows):
    vmem = pl.BlockSpec(memory_space=pltpu.VMEM)
    smem = pl.BlockSpec(memory_space=pltpu.SMEM)
    anywhere = pl.BlockSpec(memory_space=pl.ANY)
    turned = pl.pallas_call(
        kernel,
        out_shape=jax.ShapeDtypeStruct((COLS // FAM, ROWS), jnp.bfloat16),
        in_specs=[smem, smem, smem, anywhere, anywhere, anywhere],
        out_specs=vmem,
        scratch_shapes=[
            pltpu.VMEM((S, ROWS, WIDTH), jnp.bfloat16),
            pltpu.VMEM((S, ROWS, WIDTH), jnp.bfloat16),
            pltpu.VMEM((2, KMAX, ROWS, ROWS), jnp.bfloat16),
            pltpu.VMEM((1, COLS, COLS), jnp.bfloat16),
            pltpu.VMEM((COLS, COLS), jnp.bfloat16),
            pltpu.VMEM((ROWS, WIDTH), jnp.float32),
            pltpu.VMEM((COLS, ROWS), jnp.float32),
            pltpu.VMEM((2, ROWS, WIDTH), jnp.bfloat16),
            pltpu.VMEM((2, ROWS, WIDTH), jnp.bfloat16),
            pltpu.VMEM((PARTS, FAM, COLS // FAM, DEPTH), jnp.bfloat16),
            pltpu.VMEM((PARTS, FAM, COLS // FAM, DEPTH), jnp.bfloat16),
            pltpu.SemaphoreType.DMA((4,)),
            pltpu.SemaphoreType.DMA,
            pltpu.SemaphoreType.DMA((len(ROUNDS), len(LINKS))),
            pltpu.SemaphoreType.DMA,
            pltpu.SemaphoreType.DMA,
            pltpu.SemaphoreType.DMA((1 + PARTS,)),
            pltpu.SemaphoreType.DMA((1 + PARTS,)),
            pltpu.SemaphoreType.DMA,
            pltpu.SemaphoreType.DMA((PARTS,)),
        ],
        compiler_params=pltpu.CompilerParams(
            collective_id=0, has_side_effects=True, vmem_limit_bytes=56 * 2**20
        ),
        cost_estimate=pl.CostEstimate(flops=2 * KMAX * ROWS * SROW * COLS, bytes_accessed=9 * 2**20, transcendentals=0),
        name="gather_multiply_scatter",
    )(jnp.swapaxes(term_sources, 1, 2), term_counts, sector_rows, wavefunction, left_blocks, right_blocks)
    return turned.T


def solution(mesh):
    return jax.shard_map(
        body,
        mesh=mesh,
        in_specs=(
            P("owner", None),
            P("fam", None, "owner", None),
            P("fam", None, None),
            P(),
            P(),
            P(),
        ),
        out_specs=P("owner", "fam"),
        check_vma=False,
    )
```
